512 devices in a mesh: shot: 64 (over z_lo, y, x), off: 8 (over z_hi, core).
Axes of the slice: x: 4, y: 4, z: 16 (z_hi: 4, z_lo: 4; z = z_hi * 4 + z_lo), core: 2. Of those that a mesh axis runs over, the one named last changes fastest.
Arguments:
- earth_model: float32 [4096, 40], P('shot'), may hold values from -3 to 3
- layer_count: int32 [4096], P('shot'), may hold values from 20 to 40, as said below
- thickness: float32 [40], replicated, may hold values from 0.005 to 0.04
- frequency: float32 [5], replicated, may hold values from 0.5 to 4
- midpoint_shift: int32 [64], replicated, may hold values from 0 to 64, as said below
- filters: bfloat16 [201, 64], P(None, 'off'), may hold values from -0.4375 to 0.4375
- weights: bfloat16 [5, 64, 4096], P(None, 'off', 'shot'), may hold values from 0.019897461 to 0.19921875
- residual: bfloat16 [5, 64, 4096], P(None, 'off', 'shot'), may hold values from -6 to 6
Outputs:
- normal: float32 [4096, 1600], P(('shot', 'off'))
- gradient: float32 [4096, 40], P(('shot', 'off'))
The draws below stay inside these ranges and needn't reach their ends.
Inputs may be any that keep to these rules, and one draw needn't show every extreme that they name: `midpoint_shift`: nondecreasing along the offsets; the last offset's shift is exactly 64. `layer_count`: some midpoint has all 40 layers active.
All inputs are finite; a program needn't handle non-finite values.
Results may differ from the reference program's by a relative error of at most 0.003.
Values may be sent and summed in bfloat16 or wider, within the bound.
A program may use at most 192 MiB of HBM per device.

```python
import math
import jax
import jax.numpy as jnp
from jax import lax

L = 40
F = 5
NK = 201
MAXSH = 64
SHOTS = 4096
OFFSETS = 64


def draw_midpoint_shift(key, part):
    raw = jax.random.randint(key, (OFFSETS,), 0, MAXSH + 1)
    return jnp.sort(raw).at[OFFSETS - 1].set(MAXSH).astype(jnp.int32)


def draw_layer_count(key, part):
    raw = jax.random.randint(key, (SHOTS,), L // 2, L + 1)
    return raw.at[0].set(L).at[1].set(L // 2).astype(jnp.int32)


def steps_of(own_key, shape, split, least, high):
    gain, own = 1.0, jax.random.fold_in(own_key, 6)
    for axis_at, parts in split:
        heights = jnp.exp(jax.random.uniform(jax.random.fold_in(own, axis_at), (parts,), jnp.float32, least / len(split), high / len(split)))
        gain = gain * jnp.repeat(heights, shape[axis_at] // parts).reshape([-1 if axis == axis_at else 1 for axis in range(len(shape))])
    return gain


def gaussian(rng, dims, scale, reach, cuts=(), kind=jnp.bfloat16):
    array = jax.random.normal(rng, dims, jnp.float32) * scale
    if len(cuts) > 0:
        array = steps_of(rng, dims, cuts, -0.22, 0.18) * array
    return jnp.clip(array, min=-reach, max=reach).astype(kind)


def setup_inputs(seed: int = 0) -> dict:
    arg_keys = jax.random.split(jax.random.key(seed), 9)
    return {
        "earth_model": gaussian(arg_keys[0], (SHOTS, L), 0.7, 3.0, ((0, 64),), jnp.float32),
        "layer_count": draw_layer_count(jax.random.fold_in(arg_keys[8], 71), 0),
        "thickness": jnp.clip(jnp.exp(jax.random.uniform(arg_keys[2], (L,), jnp.float32, math.log(0.005), math.log(0.04))), 0.005, 0.04),
        "frequency": jnp.clip(jnp.exp(jax.random.uniform(arg_keys[3], (F,), jnp.float32, math.log(0.5), math.log(4.0))), 0.5, 4.0),
        "midpoint_shift": draw_midpoint_shift(jax.random.fold_in(arg_keys[8], 71), 0),
        "filters": gaussian(arg_keys[5], (NK, OFFSETS), NK ** -0.5, 0.4375, ((1, 8),)),
        "weights": jnp.clip(jnp.exp(math.log(0.19921875) - 2.3038113 * jax.random.uniform(arg_keys[6], (F, OFFSETS, SHOTS), jnp.float32) ** steps_of(arg_keys[6], (F, OFFSETS, SHOTS), ((1, 8), (2, 64)), -0.2, 0.2)), 0.019897461, 0.19921875).astype(jnp.bfloat16),
        "residual": gaussian(arg_keys[7], (F, OFFSETS, SHOTS), 1.0, 6.0, ((1, 8), (2, 64))),
    }


def wavenumbers(taps):
    grid = lax.iota(jnp.float32, taps)
    return jnp.exp(-3.0 + 6.0 * grid / (taps - 1))

def sensitivities(model_block, count_block, angular, thickness, wavenumber):
    conduct = jnp.exp(model_block).T[:, :, None]
    vertical = jnp.sqrt(wavenumber[None, None, :] ** 2 + angular * conduct)
    tangent = jnp.tanh(vertical * thickness[:, None, None])
    tan_rate = thickness[:, None, None] * (1.0 - tangent * tangent)
    wave_rate = angular * conduct / (2.0 * vertical)
    layer_index = lax.iota(jnp.int32, model_block.shape[1])
    bottom_layer = (layer_index[:, None] >= count_block[None, :] - 1)[:, :, None]

    def upward(impedance, inputs):
        layer_wave, layer_tan, is_bottom = inputs
        stepped = layer_wave * (impedance + layer_wave * layer_tan) / (layer_wave + impedance * layer_tan)
        return (jnp.where(is_bottom, layer_wave, stepped), impedance)
    surface_layer, below = lax.scan(upward, vertical[-1], (vertical, tangent, bottom_layer), reverse=True, unroll=8)
    adjoint = -2.0 * wavenumber / (wavenumber + surface_layer) ** 2

    def downward(adjoint_now, inputs):
        layer_wave, layer_tan, is_bottom, under, layer_rate, layer_slope = inputs
        upper_part = under + layer_wave * layer_tan
        lower_part = layer_wave + under * layer_tan
        by_wave = upper_part / lower_part + layer_wave * ((layer_tan + layer_wave * layer_slope) * lower_part - upper_part * (1.0 + under * layer_slope)) / lower_part ** 2
        by_below = layer_wave * layer_wave * (1.0 - layer_tan * layer_tan) / lower_part ** 2
        sensitivity = adjoint_now * jnp.where(is_bottom, 1.0, by_wave) * layer_rate
        return (jnp.where(is_bottom, 0.0, adjoint_now * by_below), sensitivity)
    _, result = lax.scan(downward, adjoint, (vertical, tangent, bottom_layer, below, wave_rate, tan_rate), unroll=8)
    return jnp.transpose(result, (1, 0, 2))

def augment(jacobian_matrix, row_weighting, row_data):
    extended_rows = jnp.concatenate([jacobian_matrix, row_data[:, None, :]], axis=1)
    return jnp.einsum('xer,xgr->xeg', jacobian_matrix * row_weighting[:, None, :], extended_rows, precision=lax.Precision.HIGHEST)

def reference(earth_model, layer_count, thickness, frequency, midpoint_shift, filters, weights, residual):
    wavenumber = wavenumbers(NK)
    block_size = math.gcd(SHOTS, 64)
    block_count = SHOTS // block_size
    filter_width = filters.astype(jnp.float32)

    def one_block(inputs):
        model_block, count_block, first_mid = inputs
        shot_index = first_mid + lax.iota(jnp.int32, block_size)[None, :] + midpoint_shift[:, None]
        inside = shot_index < SHOTS
        clipped = jnp.minimum(shot_index, SHOTS - 1)
        summed = jnp.zeros((block_size, L, L + 1), jnp.float32)
        for freq_index in range(F):
            kernel_lookup = sensitivities(model_block, count_block, frequency[freq_index], thickness, wavenumber).astype(jnp.bfloat16)
            jacobian_matrix = jnp.einsum('tx,get->gex', filter_width, kernel_lookup.astype(jnp.float32), precision=lax.Precision.HIGHEST)
            row_weighting = jnp.where(inside, jnp.take_along_axis(weights[freq_index], clipped, axis=1).astype(jnp.float32), 0.0).T
            row_data = jnp.where(inside, jnp.take_along_axis(residual[freq_index], clipped, axis=1).astype(jnp.float32), 0.0).T
            summed = summed + augment(jacobian_matrix, row_weighting, row_data)
        return summed
    starts = lax.iota(jnp.int32, block_count) * block_size
    stacked = lax.map(one_block, (earth_model.reshape(block_count, block_size, L), layer_count.reshape(block_count, block_size), starts))
    assembled = stacked.reshape(SHOTS, L, L + 1)
    normal = assembled[:, :, :L].reshape(SHOTS, L * L)
    gradient = assembled[:, :, L]
    return (normal, gradient)
```

```python
import functools

import jax
import jax.numpy as jnp
from jax import lax
from jax.experimental import pallas as pl
from jax.experimental.pallas import tpu as pltpu
from jax.sharding import PartitionSpec as P

MESH = pl.DeviceIdType.MESH
F32 = jnp.float32
BF16 = jnp.bfloat16
LANES = 128
SUB = 8
HALFSPACE = 64.0


def nt_dot(left, right):
    return lax.dot_general(left, right, (((1,), (1,)), ((), ())), preferred_element_type=F32)


def lane_index(rows, lanes=LANES):
    return lax.broadcasted_iota(jnp.int32, (rows, lanes), 1)


def kernel(
    model_ref,
    count_ref,
    thick_ref,
    freq_ref,
    shift_ref,
    filter_ref,
    weight_ref,
    resid_ref,
    normal_ref,
    grad_ref,
    small,
    rows,
    send_a,
    send_b,
    recv_a,
    recv_b,
    sigma_b,
    depth_b,
    part_s,
    part_g,
    sens,
    right,
    send_sem_a,
    send_sem_b,
    recv_sem_a,
    recv_sem_b,
):
    layers = model_ref.shape[0]
    freqs = weight_ref.shape[0]
    taps = filter_ref.shape[1]
    halves = -(-taps // LANES)
    shots = lax.axis_size("shot")
    offs = lax.axis_size("off")
    shot = lax.axis_index("shot")
    off = lax.axis_index("off")
    before = lax.rem(shot + shots - 1, shots)
    after = lax.rem(shot + 1, shots)
    others = [lax.rem(off + step, offs) for step in range(1, offs)]

    barrier = pltpu.get_barrier_semaphore()
    for other in others:
        pl.semaphore_signal(barrier, inc=1, device_id=(shot, other), device_id_type=MESH)
    for other in range(offs):
        pl.semaphore_signal(barrier, inc=1, device_id=(after, other), device_id_type=MESH)

    small[...] = jnp.zeros_like(small)
    block = model_ref.shape[1]
    small[0:layers, 0:block] = model_ref[...]
    small[layers : layers + 1, 0:block] = count_ref[...].astype(F32)
    small[layers + 1 : layers + 2, 0 : shift_ref.shape[1]] = shift_ref[...].astype(F32)
    small[...] = small[...].T
    own = small[pl.ds(pl.multiple_of(off * SUB, SUB), SUB), :]
    shift = own[:, layers + 1 : layers + 2].astype(jnp.int32)
    shift = jnp.broadcast_to(shift, (SUB, LANES))

    rows[...] = jnp.zeros_like(rows)
    bits = [(shift & (1 << b)) != 0 for b in range(7)]
    for q, ref in enumerate((weight_ref, resid_ref)):
        for f in range(freqs):
            x = ref[f].astype(F32)
            x = jnp.concatenate([x, jnp.zeros((SUB, LANES - x.shape[1]), F32)], axis=1)
            for b in range(7):
                x = jnp.where(bits[b], pltpu.roll(x, LANES - (1 << b), 1), x)
            rows[pl.ds(pl.multiple_of((off + f) * SUB, SUB), SUB), q * LANES : (q + 1) * LANES] = x
    by_weight = rows[:, 0:LANES].T
    by_resid = rows[:, LANES : 2 * LANES].T
    columns = filter_ref[...].astype(F32)
    columns = jnp.concatenate([columns, jnp.zeros((SUB, halves * LANES - taps), F32)], axis=1)
    columns = jnp.concatenate([columns[:, h * LANES : (h + 1) * LANES] for h in range(halves)], axis=0)
    columns = columns.astype(BF16)
    has_before = shot > 0
    for j in range(offs):
        at = slice(j * SUB, (j + 1) * SUB)
        send_a[j, 0:16] = jnp.concatenate([by_weight[at], by_resid[at]], axis=0).astype(BF16)
        send_a[j, 16:32] = columns
        at = slice(offs * SUB + j * SUB, offs * SUB + (j + 1) * SUB)
        tile = jnp.concatenate([by_weight[at], by_resid[at]], axis=0)
        send_b[j] = jnp.where(has_before, tile, 0.0).astype(BF16)

    pl.semaphore_wait(barrier, 2 * offs - 1)

    def copy_a(source, slot, device):
        return pltpu.make_async_remote_copy(
            src_ref=send_a.at[source],
            dst_ref=recv_a.at[slot],
            send_sem=send_sem_a.at[source],
            recv_sem=recv_sem_a.at[slot],
            device_id=(shot, device),
            device_id_type=MESH,
        )

    def copy_b(source, slot, device):
        return pltpu.make_async_remote_copy(
            src_ref=send_b.at[source],
            dst_ref=recv_b.at[slot],
            send_sem=send_sem_b.at[source],
            recv_sem=recv_sem_b.at[slot],
            device_id=(before, device),
            device_id_type=MESH,
        )

    for other in others:
        copy_a(other, off, other).start()
    for other in others + [off]:
        copy_b(other, off, other).start()
    recv_a[off] = send_a[off]

    layer = lane_index(SUB)
    count = jnp.broadcast_to(own[:, layers : layers + 1], (SUB, LANES)).astype(jnp.int32)
    thick = jnp.concatenate([thick_ref[...], jnp.zeros((1, LANES - layers), F32)], axis=1)
    thick = jnp.broadcast_to(thick, (SUB, LANES))
    depth = jnp.where(layer < count - 1, thick, jnp.where(layer == count - 1, HALFSPACE, 0.0))
    sigma = jnp.exp(own)
    for i in range(layers):
        sigma_b[i] = jnp.broadcast_to(sigma[:, i : i + 1], (SUB, LANES))
        depth_b[i] = jnp.broadcast_to(depth[:, i : i + 1], (SUB, LANES))
    lam = []
    for h in range(halves):
        tap = jnp.minimum(layer + h * LANES, taps - 1).astype(F32)
        lam.append(jnp.exp(-3.0 + 6.0 * tap / (taps - 1)))
    lam2 = [x * x for x in lam]
    omega = [freq_ref[f] for f in range(freqs)]
    chunks = [(f, h) for f in range(freqs) for h in range(halves)]

    def upward(step, carry):
        i = layers - 1 - step
        sig = sigma_b[i]
        thickness = depth_b[i]
        result = []
        for c, (f, h) in enumerate(chunks):
            num, den = carry[2 * c], carry[2 * c + 1]
            e1 = omega[f] * sig
            a = lam2[h] + e1
            r = lax.rsqrt(a)
            v = a * r
            t = jnp.tanh(v * thickness)
            tr = t * r
            new_num = num + (v * t) * den
            new_den = den + tr * num
            g = 1.0 - t * t
            hg = thickness * g
            part_s[i, :, c * LANES : (c + 1) * LANES] = e1 * (
                (den * new_den) * (tr + hg) + (num * new_num) * ((tr - hg) * (r * r))
            )
            part_g[i, :, c * LANES : (c + 1) * LANES] = g
            result += [new_num, new_den]
        return tuple(result)

    zero, one = jnp.zeros((SUB, LANES), F32), jnp.ones((SUB, LANES), F32)
    top = lax.fori_loop(0, layers, upward, (zero, one) * len(chunks))
    scale = []
    for c, (f, h) in enumerate(chunks):
        below = 1.0 / (lam[h] * top[2 * c + 1] + top[2 * c])
        scale.append(-lam[h] * below * below)

    def downward(pair, carry):
        i = pair * 2
        result = []
        for c in range(len(chunks)):
            at = slice(c * LANES, (c + 1) * LANES)
            first = part_s[i, :, at] * carry[c]
            now = carry[c] * part_g[i, :, at]
            second = part_s[i + 1, :, at] * now
            sens[pl.ds(pl.multiple_of(pair * 16, 16), 16), at] = jnp.concatenate(
                [first, second], axis=0
            ).astype(BF16)
            result.append(now * part_g[i + 1, :, at])
        return tuple(result)

    lax.fori_loop(0, layers // 2, downward, tuple(scale))

    for other in others:
        copy_a(other, other, other).wait_recv()
    for other in range(offs):
        copy_b(other, other, other).wait_recv()

    lane = lane_index(16)
    tiles = [recv_a[g, 0:16].astype(F32) + recv_b[g].astype(F32) for g in range(offs)]
    pairs = -(-freqs // 2)
    data = [jnp.zeros((16, LANES), F32) for _ in range(pairs)]
    for f in range(freqs):
        placed = jnp.zeros((16, LANES), F32)
        for g in range(offs):
            placed = jnp.where((lane >> 3) == g + f, tiles[g], placed)
        turn = ((f % 2) * 64 - f * SUB) % LANES
        data[f // 2] = data[f // 2] + (pltpu.roll(placed, turn, 1) if turn else placed)
    data = jnp.concatenate(data, axis=1)
    row_weight, row_data = data[0:SUB], data[SUB:16]

    gathered = [recv_a[g, 16:32].astype(F32) for g in range(offs)]
    filt = jnp.concatenate(
        [
            jnp.concatenate([x[h * SUB : (h + 1) * SUB] for x in gathered], axis=0)
            for h in range(halves)
        ],
        axis=1,
    )
    blank = jnp.zeros_like(filt)
    even = jnp.concatenate([filt, blank], axis=0).astype(BF16)
    odd = jnp.concatenate([blank, filt], axis=0).astype(BF16)
    width = halves * LANES

    jac = []
    for p in range(pairs):
        f = 2 * p
        part = nt_dot(sens[:, f * width : (f + 1) * width], even)
        if f + 1 < freqs:
            part = part + nt_dot(sens[:, (f + 1) * width : (f + 2) * width], odd)
        jac.append(part)
    size = layers * SUB
    jac = jnp.concatenate(jac, axis=1)
    cols = pairs * LANES
    weighted = (jac.reshape(layers, SUB, cols) * row_weight[None]).reshape(size, cols)
    upper = weighted.astype(BF16)
    lower = (weighted - upper.astype(F32)).astype(BF16)
    right[0:size] = jac.astype(BF16)
    pad = right.shape[0] - size
    right[size:] = jnp.concatenate([row_data, jnp.zeros((pad - SUB, cols), F32)], axis=0).astype(BF16)
    last = right.shape[0] - LANES
    product = jnp.concatenate(
        [
            nt_dot(upper, right[0:last]),
            nt_dot(upper, right[last:]) + nt_dot(lower, right[last:]),
        ],
        axis=1,
    )
    full = right.shape[0]
    keep = (lax.broadcasted_iota(jnp.int32, (SUB, full), 1) & 7) == lax.broadcasted_iota(
        jnp.int32, (SUB, full), 0
    )
    product = jnp.where(keep[None], product.reshape(layers, SUB, full), 0.0).reshape(size, full)
    product_upper = product.astype(BF16)
    product_lower = (product - product_upper.astype(F32)).astype(BF16)
    out_col = lax.broadcasted_iota(jnp.int32, (LANES, full), 0)
    in_col = lax.broadcasted_iota(jnp.int32, (LANES, full), 1) >> 3
    pick = (in_col == jnp.minimum(out_col, layers)).astype(F32).astype(BF16)
    picked = nt_dot(product_upper, pick) + nt_dot(product_lower, pick)

    lane = lane_index(SUB)
    out = [jnp.zeros((SUB, LANES), F32) for _ in range(-(-layers * layers // LANES))]
    grad = jnp.zeros((SUB, LANES), F32)
    for i in range(layers):
        row = picked[i * SUB : (i + 1) * SUB]
        tile, start = divmod(i * layers, LANES)
        turned = pltpu.roll(row, start, 1) if start else row
        out[tile] = jnp.where((lane >= start) & (lane < start + layers), turned, out[tile])
        if start + layers > LANES:
            out[tile + 1] = jnp.where(lane < start + layers - LANES, turned, out[tile + 1])
        grad = jnp.where(lane == 64 + i, row, grad)
    for tile, value in enumerate(out):
        stop = min(LANES, layers * layers - tile * LANES)
        normal_ref[:, tile * LANES : tile * LANES + stop] = value[:, :stop]
    grad_ref[...] = pltpu.roll(grad, 64, 1)[:, :layers]

    for other in others:
        copy_a(other, off, other).wait_send()
    for other in others + [off]:
        copy_b(other, off, other).wait_send()


def body(earth_model, layer_count, thickness, frequency, midpoint_shift, filters, weights, residual):
    block, layers = earth_model.shape
    taps, offsets = filters.shape
    freqs = frequency.shape[0]
    offs = lax.axis_size("off")
    width = -(-taps // LANES) * LANES
    pairs = -(-freqs // 2)
    full = -(-(layers * SUB + SUB) // LANES) * LANES
    vmem = pl.BlockSpec(memory_space=pltpu.VMEM)
    return pl.pallas_call(
        kernel,
        out_shape=(
            jax.ShapeDtypeStruct((block // offs, layers * layers), F32),
            jax.ShapeDtypeStruct((block // offs, layers), F32),
        ),
        in_specs=[vmem, vmem, vmem, pl.BlockSpec(memory_space=pltpu.SMEM), vmem, vmem, vmem, vmem],
        out_specs=(vmem, vmem),
        scratch_shapes=[
            pltpu.VMEM((LANES, LANES), F32),
            pltpu.VMEM((LANES, 2 * LANES), F32),
            pltpu.VMEM((offs, 32, LANES), BF16),
            pltpu.VMEM((offs, 16, LANES), BF16),
            pltpu.VMEM((offs, 32, LANES), BF16),
            pltpu.VMEM((offs, 16, LANES), BF16),
            pltpu.VMEM((layers, SUB, LANES), F32),
            pltpu.VMEM((layers, SUB, LANES), F32),
            pltpu.VMEM((layers, SUB, freqs * width), F32),
            pltpu.VMEM((layers, SUB, freqs * width), F32),
            pltpu.VMEM((layers * SUB, freqs * width), BF16),
            pltpu.VMEM((full, pairs * LANES), BF16),
            pltpu.SemaphoreType.DMA((offs,)),
            pltpu.SemaphoreType.DMA((offs,)),
            pltpu.SemaphoreType.DMA((offs,)),
            pltpu.SemaphoreType.DMA((offs,)),
        ],
        compiler_params=pltpu.CompilerParams(
            collective_id=0, has_side_effects=True, vmem_limit_bytes=32 * 1024 * 1024
        ),
    )(
        earth_model.T,
        layer_count.reshape(1, -1),
        thickness.reshape(1, -1),
        frequency,
        midpoint_shift.reshape(1, -1),
        filters.T,
        weights,
        residual,
    )


def solution(mesh):
    in_specs = (
        P("shot", None),
        P("shot"),
        P(),
        P(),
        P(),
        P(None, "off"),
        P(None, "off", "shot"),
        P(None, "off", "shot"),
    )
    out_specs = (P(("shot", "off"), None), P(("shot", "off"), None))
    return jax.shard_map(body, mesh=mesh, in_specs=in_specs, out_specs=out_specs, check_vma=False)
```

```python
import functools

import jax
import jax.numpy as jnp
from jax import lax
from jax.experimental import pallas as pl
from jax.experimental.pallas import tpu as pltpu
from jax.sharding import PartitionSpec as P

MESH = pl.DeviceIdType.MESH
F32 = jnp.float32
BF16 = jnp.bfloat16
LANES = 128
SUB = 8
HALFSPACE = 64.0


def nt_dot(left, right):
    return lax.dot_general(left, right, (((1,), (1,)), ((), ())), preferred_element_type=F32)


def lane_index(rows, lanes=LANES):
    return lax.broadcasted_iota(jnp.int32, (rows, lanes), 1)


def kernel(
    model_hbm,
    count_hbm,
    thick_hbm,
    freq_hbm,
    shift_hbm,
    filter_hbm,
    weight_hbm,
    resid_hbm,
    normal_ref,
    grad_ref,
    model_ref,
    count_ref,
    thick_ref,
    freq_ref,
    shift_ref,
    filter_ref,
    weight_ref,
    resid_ref,
    in_sem,
    small,
    rows,
    send_a,
    send_b,
    recv_a,
    recv_b,
    sigma_b,
    depth_b,
    part_s,
    part_g,
    sens,
    right,
    send_sem_a,
    send_sem_b,
    recv_sem_a,
    recv_sem_b,
):
    layers = model_ref.shape[0]
    freqs = weight_ref.shape[0]
    taps = filter_ref.shape[1]
    halves = -(-taps // LANES)
    shots = lax.axis_size("shot")
    offs = lax.axis_size("off")
    shot = lax.axis_index("shot")
    off = lax.axis_index("off")
    before = lax.rem(shot + shots - 1, shots)
    after = lax.rem(shot + 1, shots)
    reach = [lax.rem((off // 2 + hop) * 2 + (off + core) % 2, offs) for hop in (2, 1, 3, 0) for core in (1, 0)]
    others = reach[:-1]
    not_first, not_last = shot > 0, shot < shots - 1

    barrier = pltpu.get_barrier_semaphore()

    @pl.when(not_last)
    def _():
        for other in reach:
            pl.semaphore_signal(barrier, inc=1, device_id=(after, other), device_id_type=MESH)

    for other in others:
        pl.semaphore_signal(barrier, inc=1, device_id=(shot, other), device_id_type=MESH)

    loads = [
        pltpu.make_async_copy(source, target, in_sem.at[k])
        for k, (source, target) in enumerate(
            (
                (weight_hbm, weight_ref),
                (resid_hbm, resid_ref),
                (shift_hbm, shift_ref),
                (model_hbm, model_ref),
                (count_hbm, count_ref),
                (filter_hbm, filter_ref),
                (thick_hbm, thick_ref),
                (freq_hbm, freq_ref),
            )
        )
    ]
    for load in loads:
        load.start()

    small[...] = jnp.zeros_like(small)
    rows[...] = jnp.zeros_like(rows)
    for load in loads:
        load.wait()
    block = model_ref.shape[1]
    small[0:layers, 0:block] = model_ref[...]
    small[layers : layers + 1, 0:block] = count_ref[...].astype(F32)
    small[layers + 1 : layers + 2, 0 : shift_ref.shape[1]] = shift_ref[...].astype(F32)
    small[...] = small[...].T
    own = small[pl.ds(pl.multiple_of(off * SUB, SUB), SUB), :]
    shift = own[:, layers + 1 : layers + 2].astype(jnp.int32)
    shift = jnp.broadcast_to(shift, (SUB, LANES))

    bits = [(shift & (1 << b)) != 0 for b in range(7)]
    for q, ref in enumerate((weight_ref, resid_ref)):
        for f in range(freqs):
            x = ref[f].astype(F32)
            x = jnp.concatenate([x, jnp.zeros((SUB, LANES - x.shape[1]), F32)], axis=1)
            for b in range(7):
                x = jnp.where(bits[b], pltpu.roll(x, LANES - (1 << b), 1), x)
            rows[pl.ds(pl.multiple_of((off + f) * SUB, SUB), SUB), q * LANES : (q + 1) * LANES] = x
    by_weight = rows[:, 0:LANES].T
    by_resid = rows[:, LANES : 2 * LANES].T
    columns = filter_ref[...].astype(F32)
    columns = jnp.concatenate([columns, jnp.zeros((SUB, halves * LANES - taps), F32)], axis=1)
    columns = jnp.concatenate([columns[:, h * LANES : (h + 1) * LANES] for h in range(halves)], axis=0)
    columns = columns.astype(BF16)
    for j in range(offs):
        at = slice(j * SUB, (j + 1) * SUB)
        send_a[j, 0:16] = jnp.concatenate([by_weight[at], by_resid[at]], axis=0).astype(BF16)
        send_a[j, 16:32] = columns
        at = slice(offs * SUB + j * SUB, offs * SUB + (j + 1) * SUB)
        send_b[j] = jnp.concatenate([by_weight[at], by_resid[at]], axis=0).astype(BF16)

    @pl.when(not_first)
    def _():
        pl.semaphore_wait(barrier, 2 * offs - 1)

    @pl.when(jnp.logical_not(not_first))
    def _():
        pl.semaphore_wait(barrier, offs - 1)

    def copy_a(source, slot, device):
        return pltpu.make_async_remote_copy(
            src_ref=send_a.at[source],
            dst_ref=recv_a.at[slot],
            send_sem=send_sem_a.at[source],
            recv_sem=recv_sem_a.at[slot],
            device_id=(shot, device),
            device_id_type=MESH,
        )

    def copy_b(source, slot, device):
        return pltpu.make_async_remote_copy(
            src_ref=send_b.at[source],
            dst_ref=recv_b.at[slot],
            send_sem=send_sem_b.at[source],
            recv_sem=recv_sem_b.at[slot],
            device_id=(before, device),
            device_id_type=MESH,
        )

    @pl.when(not_first)
    def _():
        for other in reach[:2]:
            copy_b(other, off, other).start()

    for other in others[:2]:
        copy_a(other, off, other).start()

    @pl.when(not_first)
    def _():
        for other in reach[2:]:
            copy_b(other, off, other).start()

    for other in others[2:]:
        copy_a(other, off, other).start()
    recv_a[off] = send_a[off]

    layer = lane_index(SUB)
    count = jnp.broadcast_to(own[:, layers : layers + 1], (SUB, LANES)).astype(jnp.int32)
    thick = jnp.concatenate([thick_ref[...], jnp.zeros((1, LANES - layers), F32)], axis=1)
    thick = jnp.broadcast_to(thick, (SUB, LANES))
    depth = jnp.where(layer < count - 1, thick, jnp.where(layer == count - 1, HALFSPACE, 0.0))
    sigma = jnp.exp(own)
    for i in range(layers):
        sigma_b[i] = jnp.broadcast_to(sigma[:, i : i + 1], (SUB, LANES))
        depth_b[i] = jnp.broadcast_to(depth[:, i : i + 1], (SUB, LANES))
    lam = []
    for h in range(halves):
        tap = jnp.minimum(layer + h * LANES, taps - 1).astype(F32)
        lam.append(jnp.exp(-3.0 + 6.0 * tap / (taps - 1)))
    lam2 = [x * x for x in lam]
    omega = [jnp.broadcast_to(freq_ref[0:1, f : f + 1], (SUB, LANES)) for f in range(freqs)]
    chunks = [(f, h) for f in range(freqs) for h in range(halves)]

    def upward(step, carry):
        i = layers - 1 - step
        sig = sigma_b[i]
        thickness = depth_b[i]
        result = []
        for c, (f, h) in enumerate(chunks):
            num, den = carry[2 * c], carry[2 * c + 1]
            e1 = omega[f] * sig
            a = lam2[h] + e1
            r = lax.rsqrt(a)
            v = a * r
            t = jnp.tanh(v * thickness)
            tr = t * r
            new_num = num + (v * t) * den
            new_den = den + tr * num
            g = 1.0 - t * t
            hg = thickness * g
            part_s[i, :, c * LANES : (c + 1) * LANES] = e1 * (
                (den * new_den) * (tr + hg) + (num * new_num) * ((tr - hg) * (r * r))
            )
            part_g[i, :, c * LANES : (c + 1) * LANES] = g
            result += [new_num, new_den]
        return tuple(result)

    zero, one = jnp.zeros((SUB, LANES), F32), jnp.ones((SUB, LANES), F32)
    top = lax.fori_loop(0, layers, upward, (zero, one) * len(chunks))
    scale = []
    for c, (f, h) in enumerate(chunks):
        below = 1.0 / (lam[h] * top[2 * c + 1] + top[2 * c])
        scale.append(-lam[h] * below * below)

    def downward(pair, carry):
        i = pair * 2
        result = []
        for c in range(len(chunks)):
            at = slice(c * LANES, (c + 1) * LANES)
            first = part_s[i, :, at] * carry[c]
            now = carry[c] * part_g[i, :, at]
            second = part_s[i + 1, :, at] * now
            sens[pl.ds(pl.multiple_of(pair * 16, 16), 16), at] = jnp.concatenate(
                [first, second], axis=0
            ).astype(BF16)
            result.append(now * part_g[i + 1, :, at])
        return tuple(result)

    lax.fori_loop(0, layers // 2, downward, tuple(scale))

    for other in others:
        copy_a(other, other, other).wait_recv()

    @pl.when(not_last)
    def _():
        for other in reach:
            copy_b(other, other, other).wait_recv()

    @pl.when(jnp.logical_not(not_last))
    def _():
        recv_b[...] = jnp.zeros_like(recv_b)

    lane = lane_index(16)
    tiles = [recv_a[g, 0:16].astype(F32) + recv_b[g].astype(F32) for g in range(offs)]
    pairs = -(-freqs // 2)
    data = [jnp.zeros((16, LANES), F32) for _ in range(pairs)]
    for f in range(freqs):
        placed = jnp.zeros((16, LANES), F32)
        for g in range(offs):
            placed = jnp.where((lane >> 3) == g + f, tiles[g], placed)
        turn = ((f % 2) * 64 - f * SUB) % LANES
        data[f // 2] = data[f // 2] + (pltpu.roll(placed, turn, 1) if turn else placed)
    data = jnp.concatenate(data, axis=1)
    row_weight, row_data = data[0:SUB], data[SUB:16]

    gathered = [recv_a[g, 16:32].astype(F32) for g in range(offs)]
    filt = jnp.concatenate(
        [
            jnp.concatenate([x[h * SUB : (h + 1) * SUB] for x in gathered], axis=0)
            for h in range(halves)
        ],
        axis=1,
    )
    blank = jnp.zeros_like(filt)
    even = jnp.concatenate([filt, blank], axis=0).astype(BF16)
    odd = jnp.concatenate([blank, filt], axis=0).astype(BF16)
    width = halves * LANES

    jac = []
    for p in range(pairs):
        f = 2 * p
        part = nt_dot(sens[:, f * width : (f + 1) * width], even)
        if f + 1 < freqs:
            part = part + nt_dot(sens[:, (f + 1) * width : (f + 2) * width], odd)
        jac.append(part)
    size = layers * SUB
    jac = jnp.concatenate(jac, axis=1)
    cols = pairs * LANES
    weighted = (jac.reshape(layers, SUB, cols) * row_weight[None]).reshape(size, cols)
    upper = weighted.astype(BF16)
    lower = (weighted - upper.astype(F32)).astype(BF16)
    right[0:size] = jac.astype(BF16)
    pad = right.shape[0] - size
    right[size:] = jnp.concatenate([row_data, jnp.zeros((pad - SUB, cols), F32)], axis=0).astype(BF16)
    last = right.shape[0] - LANES
    product = jnp.concatenate(
        [
            nt_dot(upper, right[0:last]),
            nt_dot(upper, right[last:]) + nt_dot(lower, right[last:]),
        ],
        axis=1,
    )
    full = right.shape[0]
    keep = (lax.broadcasted_iota(jnp.int32, (SUB, full), 1) & 7) == lax.broadcasted_iota(
        jnp.int32, (SUB, full), 0
    )
    product = jnp.where(keep[None], product.reshape(layers, SUB, full), 0.0).reshape(size, full)
    product_upper = product.astype(BF16)
    product_lower = (product - product_upper.astype(F32)).astype(BF16)
    out_col = lax.broadcasted_iota(jnp.int32, (LANES, full), 0)
    in_col = lax.broadcasted_iota(jnp.int32, (LANES, full), 1) >> 3
    pick = (in_col == jnp.minimum(out_col, layers)).astype(F32).astype(BF16)
    picked = nt_dot(product_upper, pick) + nt_dot(product_lower, pick)

    lane = lane_index(SUB)
    out = [jnp.zeros((SUB, LANES), F32) for _ in range(-(-layers * layers // LANES))]
    grad = jnp.zeros((SUB, LANES), F32)
    for i in range(layers):
        row = picked[i * SUB : (i + 1) * SUB]
        tile, start = divmod(i * layers, LANES)
        turned = pltpu.roll(row, start, 1) if start else row
        out[tile] = jnp.where((lane >= start) & (lane < start + layers), turned, out[tile])
        if start + layers > LANES:
            out[tile + 1] = jnp.where(lane < start + layers - LANES, turned, out[tile + 1])
        grad = jnp.where(lane == 64 + i, row, grad)
    for tile, value in enumerate(out):
        stop = min(LANES, layers * layers - tile * LANES)
        normal_ref[:, tile * LANES : tile * LANES + stop] = value[:, :stop]
    grad_ref[...] = pltpu.roll(grad, 64, 1)[:, :layers]

    for other in others:
        copy_a(other, off, other).wait_send()

    @pl.when(not_first)
    def _():
        for other in reach:
            copy_b(other, off, other).wait_send()


def hand_over(normal_in, grad_in, normal_out, grad_out, sem):
    copies = [
        pltpu.make_async_copy(normal_in, normal_out, sem.at[0]),
        pltpu.make_async_copy(grad_in, grad_out, sem.at[1]),
    ]
    for copy in copies:
        copy.start()
    for copy in copies:
        copy.wait()


def body(earth_model, layer_count, thickness, frequency, midpoint_shift, filters, weights, residual):
    block, layers = earth_model.shape
    taps, offsets = filters.shape
    freqs = frequency.shape[0]
    offs = lax.axis_size("off")
    width = -(-taps // LANES) * LANES
    pairs = -(-freqs // 2)
    full = -(-(layers * SUB + SUB) // LANES) * LANES
    vmem = pl.BlockSpec(memory_space=pltpu.VMEM)
    operands = (
        earth_model.T,
        layer_count.reshape(1, -1),
        thickness.reshape(1, -1),
        frequency.reshape(1, -1),
        midpoint_shift.reshape(1, -1),
        filters.T,
        weights,
        residual,
    )
    operands = tuple(pltpu.with_memory_space_constraint(x, pltpu.HBM) for x in operands)
    results = pl.pallas_call(
        kernel,
        out_shape=(
            pltpu.VMEM((block // offs, layers * layers), F32),
            pltpu.VMEM((block // offs, layers), F32),
        ),
        in_specs=[pl.BlockSpec(memory_space=pltpu.HBM)] * len(operands),
        out_specs=(vmem, vmem),
        scratch_shapes=[pltpu.VMEM(x.shape, x.dtype) for x in operands]
        + [
            pltpu.SemaphoreType.DMA((len(operands),)),
            pltpu.VMEM((LANES, LANES), F32),
            pltpu.VMEM((LANES, 2 * LANES), F32),
            pltpu.VMEM((offs, 32, LANES), BF16),
            pltpu.VMEM((offs, 16, LANES), BF16),
            pltpu.VMEM((offs, 32, LANES), BF16),
            pltpu.VMEM((offs, 16, LANES), BF16),
            pltpu.VMEM((layers, SUB, LANES), F32),
            pltpu.VMEM((layers, SUB, LANES), F32),
            pltpu.VMEM((layers, SUB, freqs * width), F32),
            pltpu.VMEM((layers, SUB, freqs * width), F32),
            pltpu.VMEM((layers * SUB, freqs * width), BF16),
            pltpu.VMEM((full, pairs * LANES), BF16),
            pltpu.SemaphoreType.DMA((offs,)),
            pltpu.SemaphoreType.DMA((offs,)),
            pltpu.SemaphoreType.DMA((offs,)),
            pltpu.SemaphoreType.DMA((offs,)),
        ],
        compiler_params=pltpu.CompilerParams(
            collective_id=0, has_side_effects=True, vmem_limit_bytes=32 * 1024 * 1024
        ),
    )(*operands)
    results = tuple(pltpu.with_memory_space_constraint(x, pltpu.VMEM) for x in results)
    return pl.pallas_call(
        hand_over,
        out_shape=tuple(pltpu.HBM(x.shape, x.dtype) for x in results),
        in_specs=[vmem] * len(results),
        out_specs=(pl.BlockSpec(memory_space=pltpu.HBM),) * len(results),
        scratch_shapes=[pltpu.SemaphoreType.DMA((len(results),))],
    )(*results)


def solution(mesh):
    in_specs = (
        P("shot", None),
        P("shot"),
        P(),
        P(),
        P(),
        P(None, "off"),
        P(None, "off", "shot"),
        P(None, "off", "shot"),
    )
    out_specs = (P(("shot", "off"), None), P(("shot", "off"), None))
    return jax.shard_map(body, mesh=mesh, in_specs=in_specs, out_specs=out_specs, check_vma=False)
```

```python
import functools

import jax
import jax.numpy as jnp
from jax import lax
from jax.experimental import pallas as pl
from jax.experimental.pallas import tpu as pltpu
from jax.sharding import PartitionSpec as P

MESH = pl.DeviceIdType.MESH
F32 = jnp.float32
BF16 = jnp.bfloat16
LANES = 128
SUB = 8
HALFSPACE = 64.0


def nt_dot(left, right):
    return lax.dot_general(left, right, (((1,), (1,)), ((), ())), preferred_element_type=F32)


def lane_index(rows, lanes=LANES):
    return lax.broadcasted_iota(jnp.int32, (rows, lanes), 1)


def leads(quarter, other):
    rank = lambda q: q + (q == 2).astype(jnp.int32) - (q == 3).astype(jnp.int32)
    return rank(quarter) > rank(other)


def kernel(
    model_hbm,
    count_hbm,
    thick_hbm,
    freq_hbm,
    shift_hbm,
    filter_hbm,
    weight_hbm,
    resid_hbm,
    normal_ref,
    grad_ref,
    model_ref,
    count_ref,
    thick_ref,
    freq_ref,
    shift_ref,
    filter_ref,
    weight_ref,
    resid_ref,
    in_sem,
    small,
    rows,
    send_a,
    send_b,
    recv_a,
    recv_b,
    sigma_b,
    depth_b,
    part_s,
    part_g,
    sens,
    right,
    send_sem_a,
    send_sem_b,
    recv_sem_a,
    recv_sem_b,
):
    layers = model_ref.shape[0]
    freqs = weight_ref.shape[0]
    taps = filter_ref.shape[1]
    halves = -(-taps // LANES)
    shots = lax.axis_size("shot")
    offs = lax.axis_size("off")
    shot = lax.axis_index("shot")
    off = lax.axis_index("off")
    before = lax.rem(shot + shots - 1, shots)
    after = lax.rem(shot + 1, shots)
    block_z, core = off // 2, lax.rem(off, 2)
    sides = (lax.rem(core + 1, 2), core)
    hops = [lax.rem(block_z + hop, 4) for hop in (2, 1, 3)]
    pair = lambda quarter: [quarter * 2 + side for side in sides]
    not_first, not_last = shot > 0, shot < shots - 1
    sibling = block_z * 2 + sides[0]

    barrier = pltpu.get_barrier_semaphore()

    def announce(at_shot, device):
        pl.semaphore_signal(barrier, inc=1, device_id=(at_shot, device), device_id_type=MESH)

    for quarter in hops:

        @pl.when(leads(quarter, block_z))
        def _():
            for device in pair(quarter):
                announce(shot, device)

            @pl.when(not_last)
            def _():
                for device in pair(quarter):
                    announce(after, device)

    announce(shot, sibling)

    @pl.when(not_last)
    def _():
        for device in pair(block_z):
            announce(after, device)

    loads = [
        pltpu.make_async_copy(source, target, in_sem.at[k])
        for k, (source, target) in enumerate(
            (
                (weight_hbm, weight_ref),
                (resid_hbm, resid_ref),
                (shift_hbm, shift_ref),
                (filter_hbm, filter_ref),
                (model_hbm, model_ref),
                (count_hbm, count_ref),
                (thick_hbm, thick_ref),
                (freq_hbm, freq_ref),
            )
        )
    ]
    for load in loads:
        load.start()

    rows[...] = jnp.zeros_like(rows)
    for load in loads[:3]:
        load.wait()
    layer = lane_index(SUB)
    own_offset = layer == off * SUB + lax.broadcasted_iota(jnp.int32, (SUB, LANES), 0)
    shift = jnp.concatenate([shift_ref[...], jnp.zeros((1, LANES - shift_ref.shape[1]), jnp.int32)], axis=1)
    shift = jnp.where(own_offset, jnp.broadcast_to(shift, (SUB, LANES)).astype(F32), 0.0)
    shift = jnp.broadcast_to(jnp.sum(shift, axis=1, keepdims=True), (SUB, LANES)).astype(jnp.int32)

    bits = [(shift & (1 << b)) != 0 for b in range(7)]
    for q, ref in enumerate((weight_ref, resid_ref)):
        for f in range(freqs):
            x = ref[f].astype(F32)
            x = jnp.concatenate([x, jnp.zeros((SUB, LANES - x.shape[1]), F32)], axis=1)
            for b in range(7):
                x = jnp.where(bits[b], pltpu.roll(x, LANES - (1 << b), 1), x)
            rows[pl.ds(pl.multiple_of(lax.rem(off + f + q * 8, 16) * SUB, SUB), SUB), :] = x
    moved = rows[...].T
    loads[3].wait()
    columns = filter_ref[...].astype(F32)
    columns = jnp.concatenate([columns, jnp.zeros((SUB, halves * LANES - taps), F32)], axis=1).astype(BF16)
    for j in range(offs):
        send_a[j, 0] = moved[j * SUB : (j + 1) * SUB].astype(BF16)
        for h in range(halves):
            send_a[j, 1 + h] = columns[:, h * LANES : (h + 1) * LANES]
        send_b[j] = moved[(offs + j) * SUB : (offs + j + 1) * SUB].astype(BF16)

    led = sum(leads(block_z, quarter).astype(jnp.int32) for quarter in hops)
    pl.semaphore_wait(barrier, 2 * led + 1 + not_first.astype(jnp.int32) * (2 * led + 2))

    def copy_a(source, slot, device):
        return pltpu.make_async_remote_copy(
            src_ref=send_a.at[source],
            dst_ref=recv_a.at[slot],
            send_sem=send_sem_a.at[source],
            recv_sem=recv_sem_a.at[slot],
            device_id=(shot, device),
            device_id_type=MESH,
        )

    def copy_b(source, slot, device):
        return pltpu.make_async_remote_copy(
            src_ref=send_b.at[source],
            dst_ref=recv_b.at[slot],
            send_sem=send_sem_b.at[source],
            recv_sem=recv_sem_b.at[slot],
            device_id=(before, device),
            device_id_type=MESH,
        )

    def send_to(quarter):
        @pl.when(not_first)
        def _():
            for device in pair(quarter):
                copy_b(device, off, device).start()

        for device in pair(quarter):
            copy_a(device, off, device).start()

    for quarter in hops:

        @pl.when(leads(block_z, quarter))
        def _():
            send_to(quarter)

    @pl.when(not_first)
    def _():
        for device in pair(block_z):
            copy_b(device, off, device).start()

    copy_a(sibling, off, sibling).start()
    recv_a[off] = send_a[off]

    for load in loads[4:]:
        load.wait()
    small[...] = jnp.zeros_like(small)
    block = model_ref.shape[1]
    small[0:layers, 0:block] = model_ref[...]
    small[layers : layers + 1, 0:block] = count_ref[...].astype(F32)
    small[...] = small[...].T
    own = small[pl.ds(pl.multiple_of(off * SUB, SUB), SUB), :]

    count = jnp.broadcast_to(own[:, layers : layers + 1], (SUB, LANES)).astype(jnp.int32)
    thick = jnp.concatenate([thick_ref[...], jnp.zeros((1, LANES - layers), F32)], axis=1)
    thick = jnp.broadcast_to(thick, (SUB, LANES))
    depth = jnp.where(layer < count - 1, thick, jnp.where(layer == count - 1, HALFSPACE, 0.0))
    sigma = jnp.exp(own)
    for i in range(layers):
        sigma_b[i] = jnp.broadcast_to(sigma[:, i : i + 1], (SUB, LANES))
        depth_b[i] = jnp.broadcast_to(depth[:, i : i + 1], (SUB, LANES))
    lam = []
    for h in range(halves):
        tap = jnp.minimum(layer + h * LANES, taps - 1).astype(F32)
        lam.append(jnp.exp(-3.0 + 6.0 * tap / (taps - 1)))
    lam2 = [x * x for x in lam]
    omega = [jnp.broadcast_to(freq_ref[0:1, f : f + 1], (SUB, LANES)) for f in range(freqs)]
    chunks = [(f, h) for f in range(freqs) for h in range(halves)]

    def upward(step, carry):
        i = layers - 1 - step
        sig = sigma_b[i]
        thickness = depth_b[i]
        result = []
        for c, (f, h) in enumerate(chunks):
            num, den = carry[2 * c], carry[2 * c + 1]
            e1 = omega[f] * sig
            a = lam2[h] + e1
            r = lax.rsqrt(a)
            v = a * r
            t = jnp.tanh(v * thickness)
            tr = t * r
            new_num = num + (v * t) * den
            new_den = den + tr * num
            g = 1.0 - t * t
            hg = thickness * g
            part_s[i, :, c * LANES : (c + 1) * LANES] = e1 * (
                (den * new_den) * (tr + hg) + (num * new_num) * ((tr - hg) * (r * r))
            )
            part_g[i, :, c * LANES : (c + 1) * LANES] = g
            result += [new_num, new_den]
        return tuple(result)

    zero, one = jnp.zeros((SUB, LANES), F32), jnp.ones((SUB, LANES), F32)
    top = lax.fori_loop(0, layers, upward, (zero, one) * len(chunks))
    scale = []
    for c, (f, h) in enumerate(chunks):
        below = 1.0 / (lam[h] * top[2 * c + 1] + top[2 * c])
        scale.append(-lam[h] * below * below)

    def downward(pair, carry):
        i = pair * 2
        result = []
        for c in range(len(chunks)):
            at = slice(c * LANES, (c + 1) * LANES)
            first = part_s[i, :, at] * carry[c]
            now = carry[c] * part_g[i, :, at]
            second = part_s[i + 1, :, at] * now
            sens[pl.ds(pl.multiple_of(pair * 16, 16), 16), at] = jnp.concatenate(
                [first, second], axis=0
            ).astype(BF16)
            result.append(now * part_g[i + 1, :, at])
        return tuple(result)

    lax.fori_loop(0, layers // 2, downward, tuple(scale))

    for quarter in (hops[1], hops[2], hops[0]):
        for device in pair(quarter):
            copy_a(device, device, device).wait_recv()

        @pl.when(jnp.logical_not(leads(block_z, quarter)))
        def _():
            send_to(quarter)

    copy_a(sibling, sibling, sibling).wait_recv()

    @pl.when(not_last)
    def _():
        for quarter in [block_z] + hops:
            for device in pair(quarter):
                copy_b(device, device, device).wait_recv()

    @pl.when(jnp.logical_not(not_last))
    def _():
        recv_b[...] = jnp.zeros_like(recv_b)

    lane = lane_index(SUB)
    tiles = [recv_a[g, 0].astype(F32) + recv_b[g].astype(F32) for g in range(offs)]
    pairs = -(-freqs // 2)
    data = [[jnp.zeros((SUB, LANES), F32) for _ in range(pairs)] for _ in range(2)]
    for q in range(2):
        for f in range(freqs):
            placed = jnp.zeros((SUB, LANES), F32)
            for g in range(offs):
                placed = jnp.where((lane >> 3) == (g + f + q * 8) % 16, tiles[g], placed)
            turn = ((f % 2 + q) * 64 - f * SUB) % LANES
            data[q][f // 2] = data[q][f // 2] + (pltpu.roll(placed, turn, 1) if turn else placed)
    row_weight, row_data = (jnp.concatenate(x, axis=1) for x in data)

    gathered = [[recv_a[g, 1 + h].astype(F32) for h in range(halves)] for g in range(offs)]
    filt = jnp.concatenate(
        [
            jnp.concatenate([x[h] for x in gathered], axis=0)
            for h in range(halves)
        ],
        axis=1,
    )
    blank = jnp.zeros_like(filt)
    even = jnp.concatenate([filt, blank], axis=0).astype(BF16)
    odd = jnp.concatenate([blank, filt], axis=0).astype(BF16)
    width = halves * LANES

    jac = []
    for p in range(pairs):
        f = 2 * p
        part = nt_dot(sens[:, f * width : (f + 1) * width], even)
        if f + 1 < freqs:
            part = part + nt_dot(sens[:, (f + 1) * width : (f + 2) * width], odd)
        jac.append(part)
    size = layers * SUB
    jac = jnp.concatenate(jac, axis=1)
    cols = pairs * LANES
    weighted = (jac.reshape(layers, SUB, cols) * row_weight[None]).reshape(size, cols)
    upper = weighted.astype(BF16)
    lower = (weighted - upper.astype(F32)).astype(BF16)
    right[0:size] = jac.astype(BF16)
    pad = right.shape[0] - size
    right[size:] = jnp.concatenate([row_data, jnp.zeros((pad - SUB, cols), F32)], axis=0).astype(BF16)
    last = right.shape[0] - LANES
    product = jnp.concatenate(
        [
            nt_dot(upper, right[0:last]),
            nt_dot(upper, right[last:]) + nt_dot(lower, right[last:]),
        ],
        axis=1,
    )
    full = right.shape[0]
    keep = (lax.broadcasted_iota(jnp.int32, (SUB, full), 1) & 7) == lax.broadcasted_iota(
        jnp.int32, (SUB, full), 0
    )
    product = jnp.where(keep[None], product.reshape(layers, SUB, full), 0.0).reshape(size, full)
    product_upper = product.astype(BF16)
    product_lower = (product - product_upper.astype(F32)).astype(BF16)
    out_col = lax.broadcasted_iota(jnp.int32, (LANES, full), 0)
    in_col = lax.broadcasted_iota(jnp.int32, (LANES, full), 1) >> 3
    pick = (in_col == jnp.minimum(out_col, layers)).astype(F32).astype(BF16)
    picked = nt_dot(product_upper, pick) + nt_dot(product_lower, pick)

    lane = lane_index(SUB)
    out = [jnp.zeros((SUB, LANES), F32) for _ in range(-(-layers * layers // LANES))]
    grad = jnp.zeros((SUB, LANES), F32)
    for i in range(layers):
        row = picked[i * SUB : (i + 1) * SUB]
        tile, start = divmod(i * layers, LANES)
        turned = pltpu.roll(row, start, 1) if start else row
        out[tile] = jnp.where((lane >= start) & (lane < start + layers), turned, out[tile])
        if start + layers > LANES:
            out[tile + 1] = jnp.where(lane < start + layers - LANES, turned, out[tile + 1])
        grad = jnp.where(lane == 64 + i, row, grad)
    for tile, value in enumerate(out):
        stop = min(LANES, layers * layers - tile * LANES)
        normal_ref[:, tile * LANES : tile * LANES + stop] = value[:, :stop]
    grad_ref[...] = pltpu.roll(grad, 64, 1)[:, :layers]

    for quarter in hops:
        for device in pair(quarter):
            copy_a(device, off, device).wait_send()
    copy_a(sibling, off, sibling).wait_send()

    @pl.when(not_first)
    def _():
        for quarter in [block_z] + hops:
            for device in pair(quarter):
                copy_b(device, off, device).wait_send()


def hand_over(normal_in, grad_in, normal_out, grad_out, sem):
    copies = [
        pltpu.make_async_copy(normal_in, normal_out, sem.at[0]),
        pltpu.make_async_copy(grad_in, grad_out, sem.at[1]),
    ]
    for copy in copies:
        copy.start()
    for copy in copies:
        copy.wait()


def body(earth_model, layer_count, thickness, frequency, midpoint_shift, filters, weights, residual):
    block, layers = earth_model.shape
    taps, offsets = filters.shape
    freqs = frequency.shape[0]
    offs = lax.axis_size("off")
    width = -(-taps // LANES) * LANES
    pairs = -(-freqs // 2)
    full = -(-(layers * SUB + SUB) // LANES) * LANES
    vmem = pl.BlockSpec(memory_space=pltpu.VMEM)
    operands = (
        earth_model.T,
        layer_count.reshape(1, -1),
        thickness.reshape(1, -1),
        frequency.reshape(1, -1),
        midpoint_shift.reshape(1, -1),
        filters.T,
        weights,
        residual,
    )
    operands = tuple(pltpu.with_memory_space_constraint(x, pltpu.HBM) for x in operands)
    results = pl.pallas_call(
        kernel,
        out_shape=(
            pltpu.VMEM((block // offs, layers * layers), F32),
            pltpu.VMEM((block // offs, layers), F32),
        ),
        in_specs=[pl.BlockSpec(memory_space=pltpu.HBM)] * len(operands),
        out_specs=(vmem, vmem),
        scratch_shapes=[pltpu.VMEM(x.shape, x.dtype) for x in operands]
        + [
            pltpu.SemaphoreType.DMA((len(operands),)),
            pltpu.VMEM((LANES, LANES), F32),
            pltpu.VMEM((LANES, LANES), F32),
            pltpu.VMEM((offs, 1 + width // LANES, SUB, LANES), BF16),
            pltpu.VMEM((offs, SUB, LANES), BF16),
            pltpu.VMEM((offs, 1 + width // LANES, SUB, LANES), BF16),
            pltpu.VMEM((offs, SUB, LANES), BF16),
            pltpu.VMEM((layers, SUB, LANES), F32),
            pltpu.VMEM((layers, SUB, LANES), F32),
            pltpu.VMEM((layers, SUB, freqs * width), F32),
            pltpu.VMEM((layers, SUB, freqs * width), F32),
            pltpu.VMEM((layers * SUB, freqs * width), BF16),
            pltpu.VMEM((full, pairs * LANES), BF16),
            pltpu.SemaphoreType.DMA((offs,)),
            pltpu.SemaphoreType.DMA((offs,)),
            pltpu.SemaphoreType.DMA((offs,)),
            pltpu.SemaphoreType.DMA((offs,)),
        ],
        compiler_params=pltpu.CompilerParams(
            collective_id=0, has_side_effects=True, vmem_limit_bytes=32 * 1024 * 1024
        ),
    )(*operands)
    results = tuple(pltpu.with_memory_space_constraint(x, pltpu.VMEM) for x in results)
    return pl.pallas_call(
        hand_over,
        out_shape=tuple(pltpu.HBM(x.shape, x.dtype) for x in results),
        in_specs=[vmem] * len(results),
        out_specs=(pl.BlockSpec(memory_space=pltpu.HBM),) * len(results),
        scratch_shapes=[pltpu.SemaphoreType.DMA((len(results),))],
    )(*results)


def solution(mesh):
    in_specs = (
        P("shot", None),
        P("shot"),
        P(),
        P(),
        P(),
        P(None, "off"),
        P(None, "off", "shot"),
        P(None, "off", "shot"),
    )
    out_specs = (P(("shot", "off"), None), P(("shot", "off"), None))
    return jax.shard_map(body, mesh=mesh, in_specs=in_specs, out_specs=out_specs, check_vma=False)
```

```python
import functools

import jax
import jax.numpy as jnp
from jax import lax
from jax.experimental import pallas as pl
from jax.experimental.pallas import tpu as pltpu
from jax.sharding import PartitionSpec as P

MESH = pl.DeviceIdType.MESH
F32 = jnp.float32
BF16 = jnp.bfloat16
LANES = 128
SUB = 8
HALFSPACE = 64.0


def nt_dot(left, right):
    return lax.dot_general(left, right, (((1,), (1,)), ((), ())), preferred_element_type=F32)


def lane_index(rows, lanes=LANES):
    return lax.broadcasted_iota(jnp.int32, (rows, lanes), 1)


LEADS = 0x3bde


def leads(quarter, other):
    return ((LEADS >> (quarter * 4 + other)) & 1) != 0


def is_early(quarter):
    return quarter < 2


def kernel(
    model_hbm,
    count_hbm,
    thick_hbm,
    freq_hbm,
    shift_hbm,
    filter_hbm,
    weight_hbm,
    resid_hbm,
    normal_ref,
    grad_ref,
    model_ref,
    count_ref,
    thick_ref,
    freq_ref,
    shift_ref,
    filter_ref,
    weight_ref,
    resid_ref,
    in_sem,
    small,
    rows,
    send_a,
    send_b,
    recv_a,
    recv_b,
    sigma_b,
    depth_b,
    part_s,
    part_g,
    sens,
    right,
    send_sem_a,
    send_sem_b,
    recv_sem_a,
    recv_sem_b,
    go_sem,
):
    layers = model_ref.shape[0]
    freqs = weight_ref.shape[0]
    taps = filter_ref.shape[1]
    halves = -(-taps // LANES)
    shots = lax.axis_size("shot")
    offs = lax.axis_size("off")
    shot = lax.axis_index("shot")
    off = lax.axis_index("off")
    before = lax.rem(shot + shots - 1, shots)
    after = lax.rem(shot + 1, shots)
    block_z, core = off // 2, lax.rem(off, 2)
    sides = (lax.rem(core + 1, 2), core)
    hops = [lax.rem(block_z + hop, 4) for hop in (2, 1, 3)]
    pair = lambda quarter: [quarter * 2 + side for side in sides]
    not_first, not_last = shot > 0, shot < shots - 1
    sibling = block_z * 2 + sides[0]

    barrier = pltpu.get_barrier_semaphore()

    def announce(at_shot, device):
        pl.semaphore_signal(barrier, inc=1, device_id=(at_shot, device), device_id_type=MESH)

    for quarter in hops:

        @pl.when(leads(quarter, block_z))
        def _():
            for device in pair(quarter):
                announce(shot, device)

        @pl.when(leads(quarter, block_z) & is_early(block_z) & not_last)
        def _():
            for device in pair(quarter):
                announce(after, device)

    announce(shot, sibling)

    @pl.when(not_last)
    def _():
        for device in pair(block_z):
            announce(after, device)

    @pl.when(not_first)
    def _():
        announce(before, off)

    loads = [
        pltpu.make_async_copy(source, target, in_sem.at[k])
        for k, (source, target) in enumerate(
            (
                (weight_hbm, weight_ref),
                (resid_hbm, resid_ref),
                (shift_hbm, shift_ref),
                (filter_hbm, filter_ref),
                (model_hbm, model_ref),
                (count_hbm, count_ref),
                (thick_hbm, thick_ref),
                (freq_hbm, freq_ref),
            )
        )
    ]
    for load in loads:
        load.start()

    rows[...] = jnp.zeros_like(rows)
    for load in loads[:3]:
        load.wait()
    layer = lane_index(SUB)
    own_offset = layer == off * SUB + lax.broadcasted_iota(jnp.int32, (SUB, LANES), 0)
    shift = jnp.concatenate([shift_ref[...], jnp.zeros((1, LANES - shift_ref.shape[1]), jnp.int32)], axis=1)
    shift = jnp.where(own_offset, jnp.broadcast_to(shift, (SUB, LANES)).astype(F32), 0.0)
    shift = jnp.broadcast_to(jnp.sum(shift, axis=1, keepdims=True), (SUB, LANES)).astype(jnp.int32)

    bits = [(shift & (1 << b)) != 0 for b in range(7)]
    for q, ref in enumerate((weight_ref, resid_ref)):
        for f in range(freqs):
            x = ref[f].astype(F32)
            x = jnp.concatenate([x, jnp.zeros((SUB, LANES - x.shape[1]), F32)], axis=1)
            for b in range(7):
                x = jnp.where(bits[b], pltpu.roll(x, LANES - (1 << b), 1), x)
            rows[pl.ds(pl.multiple_of(lax.rem(off + f + q * 8, 16) * SUB, SUB), SUB), :] = x
    moved = rows[...].T
    loads[3].wait()
    columns = filter_ref[...].astype(F32)
    columns = jnp.concatenate([columns, jnp.zeros((SUB, halves * LANES - taps), F32)], axis=1).astype(BF16)
    for j in range(offs):
        send_a[j, 0] = moved[j * SUB : (j + 1) * SUB].astype(BF16)
        for h in range(halves):
            send_a[j, 1 + h] = columns[:, h * LANES : (h + 1) * LANES]
        send_b[j] = moved[(offs + j) * SUB : (offs + j + 1) * SUB].astype(BF16)

    led = sum(leads(block_z, quarter).astype(jnp.int32) for quarter in hops)
    led_early = sum((leads(block_z, quarter) & is_early(quarter)).astype(jnp.int32) for quarter in hops)
    pl.semaphore_wait(
        barrier,
        2 * led
        + 1
        + not_first.astype(jnp.int32) * (2 * led_early + 2)
        + not_last.astype(jnp.int32),
    )

    @pl.when(not_last)
    def _():
        pl.semaphore_signal(go_sem, inc=1, device_id=(after, off), device_id_type=MESH)

    def copy_a(source, slot, device):
        return pltpu.make_async_remote_copy(
            src_ref=send_a.at[source],
            dst_ref=recv_a.at[slot],
            send_sem=send_sem_a.at[source],
            recv_sem=recv_sem_a.at[slot],
            device_id=(shot, device),
            device_id_type=MESH,
        )

    def copy_b(source, slot, device):
        return pltpu.make_async_remote_copy(
            src_ref=send_b.at[source],
            dst_ref=recv_b.at[slot],
            send_sem=send_sem_b.at[source],
            recv_sem=recv_sem_b.at[slot],
            device_id=(before, device),
            device_id_type=MESH,
        )

    def send_a_to(quarter):
        for device in pair(quarter):
            copy_a(device, off, device).start()

    def send_b_to(quarter):
        for device in pair(quarter):
            copy_b(device, off, device).start()

    for quarter in hops:

        @pl.when(leads(block_z, quarter) & is_early(quarter) & not_first)
        def _():
            send_b_to(quarter)

        @pl.when(leads(block_z, quarter))
        def _():
            send_a_to(quarter)

    @pl.when(not_first)
    def _():
        for device in pair(block_z):
            copy_b(device, off, device).start()

    copy_a(sibling, off, sibling).start()
    recv_a[off] = send_a[off]

    for load in loads[4:]:
        load.wait()
    small[...] = jnp.zeros_like(small)
    block = model_ref.shape[1]
    small[0:layers, 0:block] = model_ref[...]
    small[layers : layers + 1, 0:block] = count_ref[...].astype(F32)
    small[...] = small[...].T
    own = small[pl.ds(pl.multiple_of(off * SUB, SUB), SUB), :]

    count = jnp.broadcast_to(own[:, layers : layers + 1], (SUB, LANES)).astype(jnp.int32)
    thick = jnp.concatenate([thick_ref[...], jnp.zeros((1, LANES - layers), F32)], axis=1)
    thick = jnp.broadcast_to(thick, (SUB, LANES))
    depth = jnp.where(layer < count - 1, thick, jnp.where(layer == count - 1, HALFSPACE, 0.0))
    sigma = jnp.exp(own)
    for i in range(layers):
        sigma_b[i] = jnp.broadcast_to(sigma[:, i : i + 1], (SUB, LANES))
        depth_b[i] = jnp.broadcast_to(depth[:, i : i + 1], (SUB, LANES))
    lam = []
    for h in range(halves):
        tap = jnp.minimum(layer + h * LANES, taps - 1).astype(F32)
        lam.append(jnp.exp(-3.0 + 6.0 * tap / (taps - 1)))
    lam2 = [x * x for x in lam]
    omega = [jnp.broadcast_to(freq_ref[0:1, f : f + 1], (SUB, LANES)) for f in range(freqs)]
    chunks = [(f, h) for f in range(freqs) for h in range(halves)]

    def upward(step, carry):
        i = layers - 1 - step
        sig = sigma_b[i]
        thickness = depth_b[i]
        result = []
        for c, (f, h) in enumerate(chunks):
            num, den = carry[2 * c], carry[2 * c + 1]
            e1 = omega[f] * sig
            a = lam2[h] + e1
            r = lax.rsqrt(a)
            v = a * r
            t = jnp.tanh(v * thickness)
            tr = t * r
            new_num = num + (v * t) * den
            new_den = den + tr * num
            g = 1.0 - t * t
            hg = thickness * g
            part_s[i, :, c * LANES : (c + 1) * LANES] = e1 * (
                (den * new_den) * (tr + hg) + (num * new_num) * ((tr - hg) * (r * r))
            )
            part_g[i, :, c * LANES : (c + 1) * LANES] = g
            result += [new_num, new_den]
        return tuple(result)

    zero, one = jnp.zeros((SUB, LANES), F32), jnp.ones((SUB, LANES), F32)
    top = lax.fori_loop(0, layers, upward, (zero, one) * len(chunks))
    scale = []
    for c, (f, h) in enumerate(chunks):
        below = 1.0 / (lam[h] * top[2 * c + 1] + top[2 * c])
        scale.append(-lam[h] * below * below)

    def downward(pair, carry):
        i = pair * 2
        result = []
        for c in range(len(chunks)):
            at = slice(c * LANES, (c + 1) * LANES)
            first = part_s[i, :, at] * carry[c]
            now = carry[c] * part_g[i, :, at]
            second = part_s[i + 1, :, at] * now
            sens[pl.ds(pl.multiple_of(pair * 16, 16), 16), at] = jnp.concatenate(
                [first, second], axis=0
            ).astype(BF16)
            result.append(now * part_g[i + 1, :, at])
        return tuple(result)

    lax.fori_loop(0, layers // 2, downward, tuple(scale))

    @pl.when(not_first)
    def _():
        pl.semaphore_wait(go_sem, 1)

    for quarter in hops:

        @pl.when(leads(block_z, quarter) & jnp.logical_not(is_early(quarter)) & not_first)
        def _():
            send_b_to(quarter)

    def arrived(quarter):
        for device in pair(quarter):
            copy_a(device, device, device).wait_recv()

    in_turn = (hops[1], hops[2], hops[0])
    for quarter in in_turn:

        @pl.when(jnp.logical_not(leads(block_z, quarter)))
        def _():
            arrived(quarter)
            send_a_to(quarter)

            @pl.when(not_first)
            def _():
                send_b_to(quarter)

    for quarter in in_turn:

        @pl.when(leads(block_z, quarter))
        def _():
            arrived(quarter)

    copy_a(sibling, sibling, sibling).wait_recv()

    @pl.when(not_last)
    def _():
        for quarter in [block_z] + hops:
            for device in pair(quarter):
                copy_b(device, device, device).wait_recv()

    @pl.when(jnp.logical_not(not_last))
    def _():
        recv_b[...] = jnp.zeros_like(recv_b)

    lane = lane_index(SUB)
    tiles = [recv_a[g, 0].astype(F32) + recv_b[g].astype(F32) for g in range(offs)]
    pairs = -(-freqs // 2)
    data = [[jnp.zeros((SUB, LANES), F32) for _ in range(pairs)] for _ in range(2)]
    for q in range(2):
        for f in range(freqs):
            placed = jnp.zeros((SUB, LANES), F32)
            for g in range(offs):
                placed = jnp.where((lane >> 3) == (g + f + q * 8) % 16, tiles[g], placed)
            turn = ((f % 2 + q) * 64 - f * SUB) % LANES
            data[q][f // 2] = data[q][f // 2] + (pltpu.roll(placed, turn, 1) if turn else placed)
    row_weight, row_data = (jnp.concatenate(x, axis=1) for x in data)

    gathered = [[recv_a[g, 1 + h].astype(F32) for h in range(halves)] for g in range(offs)]
    filt = jnp.concatenate(
        [
            jnp.concatenate([x[h] for x in gathered], axis=0)
            for h in range(halves)
        ],
        axis=1,
    )
    blank = jnp.zeros_like(filt)
    even = jnp.concatenate([filt, blank], axis=0).astype(BF16)
    odd = jnp.concatenate([blank, filt], axis=0).astype(BF16)
    width = halves * LANES

    jac = []
    for p in range(pairs):
        f = 2 * p
        part = nt_dot(sens[:, f * width : (f + 1) * width], even)
        if f + 1 < freqs:
            part = part + nt_dot(sens[:, (f + 1) * width : (f + 2) * width], odd)
        jac.append(part)
    size = layers * SUB
    jac = jnp.concatenate(jac, axis=1)
    cols = pairs * LANES
    weighted = (jac.reshape(layers, SUB, cols) * row_weight[None]).reshape(size, cols)
    upper = weighted.astype(BF16)
    lower = (weighted - upper.astype(F32)).astype(BF16)
    right[0:size] = jac.astype(BF16)
    pad = right.shape[0] - size
    right[size:] = jnp.concatenate([row_data, jnp.zeros((pad - SUB, cols), F32)], axis=0).astype(BF16)
    last = right.shape[0] - LANES
    product = jnp.concatenate(
        [
            nt_dot(upper, right[0:last]),
            nt_dot(upper, right[last:]) + nt_dot(lower, right[last:]),
        ],
        axis=1,
    )
    full = right.shape[0]
    keep = (lax.broadcasted_iota(jnp.int32, (SUB, full), 1) & 7) == lax.broadcasted_iota(
        jnp.int32, (SUB, full), 0
    )
    product = jnp.where(keep[None], product.reshape(layers, SUB, full), 0.0).reshape(size, full)
    product_upper = product.astype(BF16)
    product_lower = (product - product_upper.astype(F32)).astype(BF16)
    out_col = lax.broadcasted_iota(jnp.int32, (LANES, full), 0)
    in_col = lax.broadcasted_iota(jnp.int32, (LANES, full), 1) >> 3
    pick = (in_col == jnp.minimum(out_col, layers)).astype(F32).astype(BF16)
    picked = nt_dot(product_upper, pick) + nt_dot(product_lower, pick)

    lane = lane_index(SUB)
    out = [jnp.zeros((SUB, LANES), F32) for _ in range(-(-layers * layers // LANES))]
    grad = jnp.zeros((SUB, LANES), F32)
    for i in range(layers):
        row = picked[i * SUB : (i + 1) * SUB]
        tile, start = divmod(i * layers, LANES)
        turned = pltpu.roll(row, start, 1) if start else row
        out[tile] = jnp.where((lane >= start) & (lane < start + layers), turned, out[tile])
        if start + layers > LANES:
            out[tile + 1] = jnp.where(lane < start + layers - LANES, turned, out[tile + 1])
        grad = jnp.where(lane == 64 + i, row, grad)
    for tile, value in enumerate(out):
        stop = min(LANES, layers * layers - tile * LANES)
        normal_ref[:, tile * LANES : tile * LANES + stop] = value[:, :stop]
    grad_ref[...] = pltpu.roll(grad, 64, 1)[:, :layers]

    for quarter in hops:
        for device in pair(quarter):
            copy_a(device, off, device).wait_send()
    copy_a(sibling, off, sibling).wait_send()

    @pl.when(not_first)
    def _():
        for quarter in [block_z] + hops:
            for device in pair(quarter):
                copy_b(device, off, device).wait_send()


def hand_over(normal_in, grad_in, normal_out, grad_out, sem):
    copies = [
        pltpu.make_async_copy(normal_in, normal_out, sem.at[0]),
        pltpu.make_async_copy(grad_in, grad_out, sem.at[1]),
    ]
    for copy in copies:
        copy.start()
    for copy in copies:
        copy.wait()


def body(earth_model, layer_count, thickness, frequency, midpoint_shift, filters, weights, residual):
    block, layers = earth_model.shape
    taps, offsets = filters.shape
    freqs = frequency.shape[0]
    offs = lax.axis_size("off")
    width = -(-taps // LANES) * LANES
    pairs = -(-freqs // 2)
    full = -(-(layers * SUB + SUB) // LANES) * LANES
    vmem = pl.BlockSpec(memory_space=pltpu.VMEM)
    operands = (
        earth_model.T,
        layer_count.reshape(1, -1),
        thickness.reshape(1, -1),
        frequency.reshape(1, -1),
        midpoint_shift.reshape(1, -1),
        filters.T,
        weights,
        residual,
    )
    operands = tuple(pltpu.with_memory_space_constraint(x, pltpu.HBM) for x in operands)
    results = pl.pallas_call(
        kernel,
        out_shape=(
            pltpu.VMEM((block // offs, layers * layers), F32),
            pltpu.VMEM((block // offs, layers), F32),
        ),
        in_specs=[pl.BlockSpec(memory_space=pltpu.HBM)] * len(operands),
        out_specs=(vmem, vmem),
        scratch_shapes=[pltpu.VMEM(x.shape, x.dtype) for x in operands]
        + [
            pltpu.SemaphoreType.DMA((len(operands),)),
            pltpu.VMEM((LANES, LANES), F32),
            pltpu.VMEM((LANES, LANES), F32),
            pltpu.VMEM((offs, 1 + width // LANES, SUB, LANES), BF16),
            pltpu.VMEM((offs, SUB, LANES), BF16),
            pltpu.VMEM((offs, 1 + width // LANES, SUB, LANES), BF16),
            pltpu.VMEM((offs, SUB, LANES), BF16),
            pltpu.VMEM((layers, SUB, LANES), F32),
            pltpu.VMEM((layers, SUB, LANES), F32),
            pltpu.VMEM((layers, SUB, freqs * width), F32),
            pltpu.VMEM((layers, SUB, freqs * width), F32),
            pltpu.VMEM((layers * SUB, freqs * width), BF16),
            pltpu.VMEM((full, pairs * LANES), BF16),
            pltpu.SemaphoreType.DMA((offs,)),
            pltpu.SemaphoreType.DMA((offs,)),
            pltpu.SemaphoreType.DMA((offs,)),
            pltpu.SemaphoreType.DMA((offs,)),
            pltpu.SemaphoreType.REGULAR,
        ],
        compiler_params=pltpu.CompilerParams(
            collective_id=0, has_side_effects=True, vmem_limit_bytes=32 * 1024 * 1024
        ),
    )(*operands)
    results = tuple(pltpu.with_memory_space_constraint(x, pltpu.VMEM) for x in results)
    return pl.pallas_call(
        hand_over,
        out_shape=tuple(pltpu.HBM(x.shape, x.dtype) for x in results),
        in_specs=[vmem] * len(results),
        out_specs=(pl.BlockSpec(memory_space=pltpu.HBM),) * len(results),
        scratch_shapes=[pltpu.SemaphoreType.DMA((len(results),))],
    )(*results)


def solution(mesh):
    in_specs = (
        P("shot", None),
        P("shot"),
        P(),
        P(),
        P(),
        P(None, "off"),
        P(None, "off", "shot"),
        P(None, "off", "shot"),
    )
    out_specs = (P(("shot", "off"), None), P(("shot", "off"), None))
    return jax.shard_map(body, mesh=mesh, in_specs=in_specs, out_specs=out_specs, check_vma=False)
```

```python
import functools

import jax
import jax.numpy as jnp
from jax import lax
from jax.experimental import pallas as pl
from jax.experimental.pallas import tpu as pltpu
from jax.sharding import PartitionSpec as P

MESH = pl.DeviceIdType.MESH
F32 = jnp.float32
BF16 = jnp.bfloat16
LANES = 128
SUB = 8
HALFSPACE = 64.0


def nt_dot(left, right):
    return lax.dot_general(left, right, (((1,), (1,)), ((), ())), preferred_element_type=F32)


def lane_index(rows, lanes=LANES):
    return lax.broadcasted_iota(jnp.int32, (rows, lanes), 1)


def is_early(quarter):
    return quarter < 2


def kernel(
    model_hbm,
    count_hbm,
    thick_hbm,
    freq_hbm,
    shift_hbm,
    filter_hbm,
    weight_hbm,
    resid_hbm,
    normal_ref,
    grad_ref,
    model_ref,
    count_ref,
    thick_ref,
    freq_ref,
    shift_ref,
    filter_ref,
    weight_ref,
    resid_ref,
    in_sem,
    small,
    rows,
    send_a,
    send_b,
    recv_a,
    recv_b,
    sigma_b,
    depth_b,
    part_s,
    part_g,
    sens,
    right,
    send_sem_a,
    send_sem_b,
    recv_sem_a,
    recv_sem_b,
    go_sem,
):
    layers = model_ref.shape[0]
    freqs = weight_ref.shape[0]
    taps = filter_ref.shape[1]
    halves = -(-taps // LANES)
    shots = lax.axis_size("shot")
    offs = lax.axis_size("off")
    shot = lax.axis_index("shot")
    off = lax.axis_index("off")
    before = lax.rem(shot + shots - 1, shots)
    after = lax.rem(shot + 1, shots)
    block_z, core = off // 2, lax.rem(off, 2)
    sides = (lax.rem(core + 1, 2), core)
    hops = [lax.rem(block_z + hop, 4) for hop in (2, 1, 3)]
    pair = lambda quarter: [quarter * 2 + side for side in sides]
    not_first, not_last = shot > 0, shot < shots - 1
    sibling = block_z * 2 + sides[0]

    barrier = pltpu.get_barrier_semaphore()

    def announce(at_shot, device):
        pl.semaphore_signal(barrier, inc=1, device_id=(at_shot, device), device_id_type=MESH)

    for quarter in hops:
        for device in pair(quarter):
            announce(shot, device)
    announce(shot, sibling)

    @pl.when(not_last & is_early(block_z))
    def _():
        for quarter in hops + [block_z]:
            for device in pair(quarter):
                announce(after, device)

    @pl.when(not_first)
    def _():
        announce(before, off)

    loads = [
        pltpu.make_async_copy(source, target, in_sem.at[k])
        for k, (source, target) in enumerate(
            (
                (weight_hbm, weight_ref),
                (resid_hbm, resid_ref),
                (shift_hbm, shift_ref),
                (filter_hbm, filter_ref),
                (model_hbm, model_ref),
                (count_hbm, count_ref),
                (thick_hbm, thick_ref),
                (freq_hbm, freq_ref),
            )
        )
    ]
    for load in loads:
        load.start()

    rows[...] = jnp.zeros_like(rows)
    for load in loads[:3]:
        load.wait()
    layer = lane_index(SUB)
    own_offset = layer == off * SUB + lax.broadcasted_iota(jnp.int32, (SUB, LANES), 0)
    shift = jnp.concatenate([shift_ref[...], jnp.zeros((1, LANES - shift_ref.shape[1]), jnp.int32)], axis=1)
    shift = jnp.where(own_offset, jnp.broadcast_to(shift, (SUB, LANES)).astype(F32), 0.0)
    shift = jnp.broadcast_to(jnp.sum(shift, axis=1, keepdims=True), (SUB, LANES)).astype(jnp.int32)

    bits = [(shift & (1 << b)) != 0 for b in range(7)]
    for q, ref in enumerate((weight_ref, resid_ref)):
        for f in range(freqs):
            x = ref[f].astype(F32)
            x = jnp.concatenate([x, jnp.zeros((SUB, LANES - x.shape[1]), F32)], axis=1)
            for b in range(7):
                x = jnp.where(bits[b], pltpu.roll(x, LANES - (1 << b), 1), x)
            rows[pl.ds(pl.multiple_of(lax.rem(off + f + q * 8, 16) * SUB, SUB), SUB), :] = x
    moved = rows[...].T
    loads[3].wait()
    columns = filter_ref[...].astype(F32)
    columns = jnp.concatenate([columns, jnp.zeros((SUB, halves * LANES - taps), F32)], axis=1).astype(BF16)
    for j in range(offs):
        send_a[j, 0] = moved[j * SUB : (j + 1) * SUB].astype(BF16)
        for h in range(halves):
            send_a[j, 1 + h] = columns[:, h * LANES : (h + 1) * LANES]
        send_b[j] = moved[(offs + j) * SUB : (offs + j + 1) * SUB].astype(BF16)

    pl.semaphore_wait(
        barrier, offs - 1 + not_first.astype(jnp.int32) * (offs // 2) + not_last.astype(jnp.int32)
    )

    @pl.when(not_last)
    def _():
        pl.semaphore_signal(go_sem, inc=1, device_id=(after, off), device_id_type=MESH)

    def copy_a(source, slot, device):
        return pltpu.make_async_remote_copy(
            src_ref=send_a.at[source],
            dst_ref=recv_a.at[slot],
            send_sem=send_sem_a.at[source],
            recv_sem=recv_sem_a.at[slot],
            device_id=(shot, device),
            device_id_type=MESH,
        )

    def copy_b(source, slot, device):
        return pltpu.make_async_remote_copy(
            src_ref=send_b.at[source],
            dst_ref=recv_b.at[slot],
            send_sem=send_sem_b.at[source],
            recv_sem=recv_sem_b.at[slot],
            device_id=(before, device),
            device_id_type=MESH,
        )

    def send_a_to(quarter):
        for device in pair(quarter):
            copy_a(device, off, device).start()

    def send_b_to(quarter):
        for device in pair(quarter):
            copy_b(device, off, device).start()

    for quarter in hops:

        @pl.when(is_early(quarter) & not_first)
        def _():
            send_b_to(quarter)

        send_a_to(quarter)

    @pl.when(is_early(block_z) & not_first)
    def _():
        send_b_to(block_z)

    copy_a(sibling, off, sibling).start()
    recv_a[off] = send_a[off]

    for load in loads[4:]:
        load.wait()
    small[...] = jnp.zeros_like(small)
    block = model_ref.shape[1]
    small[0:layers, 0:block] = model_ref[...]
    small[layers : layers + 1, 0:block] = count_ref[...].astype(F32)
    small[...] = small[...].T
    own = small[pl.ds(pl.multiple_of(off * SUB, SUB), SUB), :]

    count = jnp.broadcast_to(own[:, layers : layers + 1], (SUB, LANES)).astype(jnp.int32)
    thick = jnp.concatenate([thick_ref[...], jnp.zeros((1, LANES - layers), F32)], axis=1)
    thick = jnp.broadcast_to(thick, (SUB, LANES))
    depth = jnp.where(layer < count - 1, thick, jnp.where(layer == count - 1, HALFSPACE, 0.0))
    sigma = jnp.exp(own)
    for i in range(layers):
        sigma_b[i] = jnp.broadcast_to(sigma[:, i : i + 1], (SUB, LANES))
        depth_b[i] = jnp.broadcast_to(depth[:, i : i + 1], (SUB, LANES))
    lam = []
    for h in range(halves):
        tap = jnp.minimum(layer + h * LANES, taps - 1).astype(F32)
        lam.append(jnp.exp(-3.0 + 6.0 * tap / (taps - 1)))
    lam2 = [x * x for x in lam]
    omega = [jnp.broadcast_to(freq_ref[0:1, f : f + 1], (SUB, LANES)) for f in range(freqs)]
    chunks = [(f, h) for f in range(freqs) for h in range(halves)]

    def upward(step, carry):
        i = layers - 1 - step
        sig = sigma_b[i]
        thickness = depth_b[i]
        result = []
        for c, (f, h) in enumerate(chunks):
            num, den = carry[2 * c], carry[2 * c + 1]
            e1 = omega[f] * sig
            a = lam2[h] + e1
            r = lax.rsqrt(a)
            v = a * r
            t = jnp.tanh(v * thickness)
            tr = t * r
            new_num = num + (v * t) * den
            new_den = den + tr * num
            g = 1.0 - t * t
            hg = thickness * g
            part_s[i, :, c * LANES : (c + 1) * LANES] = e1 * (
                (den * new_den) * (tr + hg) + (num * new_num) * ((tr - hg) * (r * r))
            )
            part_g[i, :, c * LANES : (c + 1) * LANES] = g
            result += [new_num, new_den]
        return tuple(result)

    zero, one = jnp.zeros((SUB, LANES), F32), jnp.ones((SUB, LANES), F32)
    top = lax.fori_loop(0, layers, upward, (zero, one) * len(chunks))
    scale = []
    for c, (f, h) in enumerate(chunks):
        below = 1.0 / (lam[h] * top[2 * c + 1] + top[2 * c])
        scale.append(-lam[h] * below * below)

    def downward(pair, carry):
        i = pair * 2
        result = []
        for c in range(len(chunks)):
            at = slice(c * LANES, (c + 1) * LANES)
            first = part_s[i, :, at] * carry[c]
            now = carry[c] * part_g[i, :, at]
            second = part_s[i + 1, :, at] * now
            sens[pl.ds(pl.multiple_of(pair * 16, 16), 16), at] = jnp.concatenate(
                [first, second], axis=0
            ).astype(BF16)
            result.append(now * part_g[i + 1, :, at])
        return tuple(result)

    lax.fori_loop(0, layers // 2, downward, tuple(scale))

    @pl.when(not_first)
    def _():
        pl.semaphore_wait(go_sem, 1)

    for quarter in [block_z] + hops:

        @pl.when(jnp.logical_not(is_early(quarter)) & not_first)
        def _():
            send_b_to(quarter)

    for quarter in hops:
        for device in pair(quarter):
            copy_a(device, device, device).wait_recv()
    copy_a(sibling, sibling, sibling).wait_recv()

    @pl.when(not_last)
    def _():
        for quarter in [block_z] + hops:
            for device in pair(quarter):
                copy_b(device, device, device).wait_recv()

    @pl.when(jnp.logical_not(not_last))
    def _():
        recv_b[...] = jnp.zeros_like(recv_b)

    lane = lane_index(SUB)
    tiles = [recv_a[g, 0].astype(F32) + recv_b[g].astype(F32) for g in range(offs)]
    pairs = -(-freqs // 2)
    data = [[jnp.zeros((SUB, LANES), F32) for _ in range(pairs)] for _ in range(2)]
    for q in range(2):
        for f in range(freqs):
            placed = jnp.zeros((SUB, LANES), F32)
            for g in range(offs):
                placed = jnp.where((lane >> 3) == (g + f + q * 8) % 16, tiles[g], placed)
            turn = ((f % 2 + q) * 64 - f * SUB) % LANES
            data[q][f // 2] = data[q][f // 2] + (pltpu.roll(placed, turn, 1) if turn else placed)
    row_weight, row_data = (jnp.concatenate(x, axis=1) for x in data)

    gathered = [[recv_a[g, 1 + h].astype(F32) for h in range(halves)] for g in range(offs)]
    filt = jnp.concatenate(
        [
            jnp.concatenate([x[h] for x in gathered], axis=0)
            for h in range(halves)
        ],
        axis=1,
    )
    blank = jnp.zeros_like(filt)
    even = jnp.concatenate([filt, blank], axis=0).astype(BF16)
    odd = jnp.concatenate([blank, filt], axis=0).astype(BF16)
    width = halves * LANES

    jac = []
    for p in range(pairs):
        f = 2 * p
        part = nt_dot(sens[:, f * width : (f + 1) * width], even)
        if f + 1 < freqs:
            part = part + nt_dot(sens[:, (f + 1) * width : (f + 2) * width], odd)
        jac.append(part)
    size = layers * SUB
    jac = jnp.concatenate(jac, axis=1)
    cols = pairs * LANES
    weighted = (jac.reshape(layers, SUB, cols) * row_weight[None]).reshape(size, cols)
    upper = weighted.astype(BF16)
    lower = (weighted - upper.astype(F32)).astype(BF16)
    right[0:size] = jac.astype(BF16)
    pad = right.shape[0] - size
    right[size:] = jnp.concatenate([row_data, jnp.zeros((pad - SUB, cols), F32)], axis=0).astype(BF16)
    last = right.shape[0] - LANES
    product = jnp.concatenate(
        [
            nt_dot(upper, right[0:last]),
            nt_dot(upper, right[last:]) + nt_dot(lower, right[last:]),
        ],
        axis=1,
    )
    full = right.shape[0]
    keep = (lax.broadcasted_iota(jnp.int32, (SUB, full), 1) & 7) == lax.broadcasted_iota(
        jnp.int32, (SUB, full), 0
    )
    product = jnp.where(keep[None], product.reshape(layers, SUB, full), 0.0).reshape(size, full)
    product_upper = product.astype(BF16)
    product_lower = (product - product_upper.astype(F32)).astype(BF16)
    out_col = lax.broadcasted_iota(jnp.int32, (LANES, full), 0)
    in_col = lax.broadcasted_iota(jnp.int32, (LANES, full), 1) >> 3
    pick = (in_col == jnp.minimum(out_col, layers)).astype(F32).astype(BF16)
    picked = nt_dot(product_upper, pick) + nt_dot(product_lower, pick)

    lane = lane_index(SUB)
    out = [jnp.zeros((SUB, LANES), F32) for _ in range(-(-layers * layers // LANES))]
    grad = jnp.zeros((SUB, LANES), F32)
    for i in range(layers):
        row = picked[i * SUB : (i + 1) * SUB]
        tile, start = divmod(i * layers, LANES)
        turned = pltpu.roll(row, start, 1) if start else row
        out[tile] = jnp.where((lane >= start) & (lane < start + layers), turned, out[tile])
        if start + layers > LANES:
            out[tile + 1] = jnp.where(lane < start + layers - LANES, turned, out[tile + 1])
        grad = jnp.where(lane == 64 + i, row, grad)
    for tile, value in enumerate(out):
        stop = min(LANES, layers * layers - tile * LANES)
        normal_ref[:, tile * LANES : tile * LANES + stop] = value[:, :stop]
    grad_ref[...] = pltpu.roll(grad, 64, 1)[:, :layers]

    for quarter in hops:
        for device in pair(quarter):
            copy_a(device, off, device).wait_send()
    copy_a(sibling, off, sibling).wait_send()

    @pl.when(not_first)
    def _():
        for quarter in [block_z] + hops:
            for device in pair(quarter):
                copy_b(device, off, device).wait_send()


def hand_over(normal_in, grad_in, normal_out, grad_out, sem):
    copies = [
        pltpu.make_async_copy(normal_in, normal_out, sem.at[0]),
        pltpu.make_async_copy(grad_in, grad_out, sem.at[1]),
    ]
    for copy in copies:
        copy.start()
    for copy in copies:
        copy.wait()


def body(earth_model, layer_count, thickness, frequency, midpoint_shift, filters, weights, residual):
    block, layers = earth_model.shape
    taps, offsets = filters.shape
    freqs = frequency.shape[0]
    offs = lax.axis_size("off")
    width = -(-taps // LANES) * LANES
    pairs = -(-freqs // 2)
    full = -(-(layers * SUB + SUB) // LANES) * LANES
    vmem = pl.BlockSpec(memory_space=pltpu.VMEM)
    operands = (
        earth_model.T,
        layer_count.reshape(1, -1),
        thickness.reshape(1, -1),
        frequency.reshape(1, -1),
        midpoint_shift.reshape(1, -1),
        filters.T,
        weights,
        residual,
    )
    operands = tuple(pltpu.with_memory_space_constraint(x, pltpu.HBM) for x in operands)
    results = pl.pallas_call(
        kernel,
        out_shape=(
            pltpu.VMEM((block // offs, layers * layers), F32),
            pltpu.VMEM((block // offs, layers), F32),
        ),
        in_specs=[pl.BlockSpec(memory_space=pltpu.HBM)] * len(operands),
        out_specs=(vmem, vmem),
        scratch_shapes=[pltpu.VMEM(x.shape, x.dtype) for x in operands]
        + [
            pltpu.SemaphoreType.DMA((len(operands),)),
            pltpu.VMEM((LANES, LANES), F32),
            pltpu.VMEM((LANES, LANES), F32),
            pltpu.VMEM((offs, 1 + width // LANES, SUB, LANES), BF16),
            pltpu.VMEM((offs, SUB, LANES), BF16),
            pltpu.VMEM((offs, 1 + width // LANES, SUB, LANES), BF16),
            pltpu.VMEM((offs, SUB, LANES), BF16),
            pltpu.VMEM((layers, SUB, LANES), F32),
            pltpu.VMEM((layers, SUB, LANES), F32),
            pltpu.VMEM((layers, SUB, freqs * width), F32),
            pltpu.VMEM((layers, SUB, freqs * width), F32),
            pltpu.VMEM((layers * SUB, freqs * width), BF16),
            pltpu.VMEM((full, pairs * LANES), BF16),
            pltpu.SemaphoreType.DMA((offs,)),
            pltpu.SemaphoreType.DMA((offs,)),
            pltpu.SemaphoreType.DMA((offs,)),
            pltpu.SemaphoreType.DMA((offs,)),
            pltpu.SemaphoreType.REGULAR,
        ],
        compiler_params=pltpu.CompilerParams(
            collective_id=0, has_side_effects=True, vmem_limit_bytes=32 * 1024 * 1024
        ),
    )(*operands)
    results = tuple(pltpu.with_memory_space_constraint(x, pltpu.VMEM) for x in results)
    return pl.pallas_call(
        hand_over,
        out_shape=tuple(pltpu.HBM(x.shape, x.dtype) for x in results),
        in_specs=[vmem] * len(results),
        out_specs=(pl.BlockSpec(memory_space=pltpu.HBM),) * len(results),
        scratch_shapes=[pltpu.SemaphoreType.DMA((len(results),))],
    )(*results)


def solution(mesh):
    in_specs = (
        P("shot", None),
        P("shot"),
        P(),
        P(),
        P(),
        P(None, "off"),
        P(None, "off", "shot"),
        P(None, "off", "shot"),
    )
    out_specs = (P(("shot", "off"), None), P(("shot", "off"), None))
    return jax.shard_map(body, mesh=mesh, in_specs=in_specs, out_specs=out_specs, check_vma=False)
```
